128 devices in a mesh: grp: 4 (over y), sub: 32 (over z, x, core).
Axes of the slice: x: 4, y: 4, z: 4, core: 2. Of those that a mesh axis runs over, the one named last changes fastest.
Arguments:
- pulses: bfloat16 [4, 32, 128, 32768], P('grp', None, None, 'sub'), may hold values from -6 to 6
- footprint: int32 [32, 2], replicated, may hold values from 0 to 31, as said below
- proj_weight: bfloat16 [32, 48, 256], replicated, may hold values from -0.375 to 0.375
- bank: bfloat16 [8, 512, 512], replicated, may hold values from -0.1875 to 0.1875
- merge_index: int32 [3, 4, 32, 64, 2], P(None, 'grp'), may hold values from 0 to 7
Outputs:
- slab: bfloat16 [1536, 32768], P('sub', 'grp')
The draws below stay inside these ranges and needn't reach their ends.
Inputs may be any that keep to these rules, and one draw needn't show every extreme that they name: `footprint`: owner o's first entry is block o; its second is another block, different from o.
All inputs are finite; a program needn't handle non-finite values.
Results may differ from the reference program's by a relative error of at most 0.0064.
Values may be sent and summed in bfloat16 or wider, within the bound.
No kernel may reach another device: no remote copies, remote signals or barrier semaphores. Data moves between devices by JAX's collectives and lax.ppermute only.
A program may use at most 256 MiB of HBM per device.

```python
import jax
import jax.numpy as jnp
from jax import lax

COLS = 32768
BLK = 256
PB = 128
KB = 8
LEVELS = 3
S = 48
BLOCKS = 32
NB = 64
N_GRP = 4
N_SUB = 32


def draw_footprint(key, part):
    key = jax.random.fold_in(key, 11)
    offset = jax.random.randint(key, (N_SUB,), 1, BLOCKS)
    owned = jnp.arange(N_SUB, dtype=jnp.int32)
    second = (owned + offset) % BLOCKS
    return jnp.stack([owned, second], axis=1).astype(jnp.int32)


def with_ends(array, own_key, least, top_value):
    place = [jax.random.randint(jax.random.fold_in(own_key, axis), (), 0, length) for axis, length in enumerate(array.shape)]
    main_axis = array.shape.index(max(array.shape))
    neighbour = place[:main_axis] + [(place[main_axis] + 1) % array.shape[main_axis]] + place[main_axis + 1:]
    return array.at[tuple(place)].set(least).at[tuple(neighbour)].set(top_value)


def steps_of(stream_key, dims, pieces, smallest, largest):
    level = 1.0
    for axis_at, parts in pieces:
        heights = jax.random.uniform(jax.random.fold_in(jax.random.fold_in(stream_key, 6), axis_at), (parts,), jnp.float32, smallest / len(pieces), largest / len(pieces))
        level = level * jnp.repeat(jnp.exp(heights), dims[axis_at] // parts).reshape((-1,) + (1,) * (len(dims) - 1 - axis_at))
    return level


def scatter_about(rng, extent, width, most, cuts=(), held_as=jnp.bfloat16):
    factor_of = steps_of(rng, extent, cuts, -0.22, 0.18) if cuts else 1.0
    array = jax.random.normal(rng, extent, jnp.float32) * width * factor_of
    return jnp.minimum(jnp.maximum(array, -most), most).astype(held_as)


def setup_inputs(seed: int = 0) -> dict:
    streams_of = jax.random.split(jax.random.key(seed), 6)
    return {
        "pulses": scatter_about(streams_of[0], (N_GRP, BLOCKS, PB, COLS), 1.0, 6.0, ((0, 4), (3, 32))),
        "footprint": draw_footprint(jax.random.fold_in(streams_of[5], 71), 0),
        "proj_weight": scatter_about(streams_of[2], (N_SUB, S, 2 * PB), (2 * PB) ** -0.5, 0.375),
        "bank": scatter_about(streams_of[3], (KB, 2 * BLK, 2 * BLK), (4 * BLK) ** -0.5, 0.1875),
        "merge_index": with_ends(jax.random.randint(streams_of[4], (LEVELS, N_GRP, N_SUB, NB, 2), 0, KB), jax.random.fold_in(streams_of[4], 1), 0, KB - 1).astype(jnp.int32),
    }


def merge_pair(own_image, partner_image, index_table, bank):
    block_width = bank.shape[1]
    beam_count = own_image.shape[0]
    block_count = own_image.shape[1] // block_width
    own_blocks = own_image.reshape(beam_count, block_count, block_width).astype(jnp.float32)
    partner_blocks = partner_image.reshape(beam_count, block_count, block_width).astype(jnp.float32)
    self_mats = jnp.take(bank, index_table[:, 0], axis=0).astype(jnp.float32)
    cross_mats = jnp.take(bank, index_table[:, 1], axis=0).astype(jnp.float32)
    merged = jnp.einsum("sbk,bkj->sbj", own_blocks, self_mats)
    merged = merged + jnp.einsum("sbk,bkj->sbj", partner_blocks, cross_mats)
    return merged.reshape(beam_count, block_count * block_width)


def group_tree(group_pulses, group_index, footprint, proj_weight, bank):
    def initial(owner):
        picked = jnp.take(group_pulses, footprint[owner], axis=0).reshape(2 * PB, COLS)
        return jnp.dot(proj_weight[owner], picked, preferred_element_type=jnp.float32).astype(jnp.bfloat16)

    owners = jnp.arange(N_SUB, dtype=jnp.int32)
    images = lax.map(initial, owners)
    for section_level in range(LEVELS):
        partners = jnp.take(images, jnp.bitwise_xor(owners, 2 ** section_level), axis=0)

        def merge_one(triple):
            return merge_pair(triple[0], triple[1], triple[2], bank)

        merged = lax.map(merge_one, (images, partners, group_index[section_level]))
        if section_level + 1 < LEVELS:
            images = merged.astype(jnp.bfloat16)
        else:
            images = merged
    return images


def reference(pulses, footprint, proj_weight, bank, merge_index):
    total = jnp.zeros((N_SUB, S, COLS), jnp.float32)
    for group_at in range(N_GRP):
        total = total + group_tree(pulses[group_at], merge_index[:, group_at], footprint, proj_weight, bank)
    return total.reshape(N_SUB * S, COLS).astype(jnp.bfloat16)
```

```python
import functools
import jax
import jax.numpy as jnp
from jax import lax
from jax.sharding import PartitionSpec as P
from jax.experimental import pallas as pl
from jax.experimental.pallas import tpu as pltpu

def merge_tree(levels, blocks, pick_ref, foot_ref, table_ref, pulses_ref, w0_ref, w1_ref, bank_ref,
               out0_ref, out1_ref, rows, mats, image, row_sem, mat_sem):
    step = pl.program_id(0)
    steps = pl.num_programs(0)
    w_refs, out_refs = (w0_ref, w1_ref), (out0_ref, out1_ref)
    members = w0_ref.shape[0]
    beams = w0_ref.shape[1]
    pulse_block = pulses_ref.shape[1]
    width = bank_ref.shape[1]
    owners = foot_ref.shape[0] // 2

    def fetches(at, slot):
        copies = []
        for b in range(blocks):
            for j in range(members):
                owner = pick_ref[at * blocks + b] * members + j
                for h in range(2):
                    copies.append(pltpu.make_async_copy(
                        pulses_ref.at[foot_ref[owner * 2 + h], :, pl.ds(b * width, width)],
                        rows.at[slot, b, j, pl.ds(h * pulse_block, pulse_block), :],
                        row_sem.at[slot, b, j, h]))
        return copies

    bank_copies = [pltpu.make_async_copy(bank_ref.at[k], mats.at[k], mat_sem.at[k]) for k in range(bank_ref.shape[0])]

    @pl.when(step == 0)
    def _():
        for c in fetches(0, 0):
            c.start()
        for c in bank_copies:
            c.start()

    slot = lax.rem(step, 2)

    @pl.when(step + 1 < steps)
    def _():
        for c in fetches(step + 1, 1 - slot):
            c.start()

    for c in fetches(step, slot):
        c.wait()
    for b in range(blocks):
        for j in range(members):
            image[0, b, j] = jnp.dot(w_refs[b][j], rows[slot, b, j], preferred_element_type=jnp.float32).astype(jnp.bfloat16)

    @pl.when(step == 0)
    def _():
        for c in bank_copies:
            c.wait()

    for level in range(levels):
        now, later = level % 2, (level + 1) % 2
        for b in range(blocks):
            for j in range(members):
                owner = pick_ref[step * blocks + b] * members + j
                at = ((level * owners + owner) * blocks + b) * 2
                acc = jnp.dot(image[now, b, j], mats[table_ref[at]], preferred_element_type=jnp.float32)
                acc = acc + jnp.dot(image[now, b, j ^ (1 << level)], mats[table_ref[at + 1]], preferred_element_type=jnp.float32)
                if level + 1 < levels:
                    image[later, b, j] = acc.astype(jnp.bfloat16)
                else:
                    out_refs[b][j % 4, 0, pl.ds((j // 4) * beams, beams), :] = acc.astype(jnp.bfloat16)


def images_of(pulses, foot, table, weight, bank, pick, levels, members=8):
    steps = pick.shape[0] // 2
    kb, width, _ = bank.shape
    owners, beams, depth = weight.shape
    blocks = pulses.shape[2] // width
    wspec = lambda b: pl.BlockSpec((members, beams, depth), lambda i, pk, ft, tb: (pk[i * blocks + b], 0, 0))
    ospec = pl.BlockSpec((4, 1, members // 4 * beams, width), lambda i, pk, ft, tb: (0, i, 0, 0))
    return pl.pallas_call(
        functools.partial(merge_tree, levels, blocks),
        grid_spec=pltpu.PrefetchScalarGridSpec(
            num_scalar_prefetch=3,
            grid=(steps,),
            in_specs=[pl.BlockSpec(memory_space=pl.ANY), wspec(0), wspec(1), pl.BlockSpec(memory_space=pl.ANY)],
            out_specs=[ospec, ospec],
            scratch_shapes=[
                pltpu.VMEM((2, blocks, members, depth, width), jnp.bfloat16),
                pltpu.VMEM((kb, width, width), jnp.bfloat16),
                pltpu.VMEM((2, blocks, members, beams, width), jnp.bfloat16),
                pltpu.SemaphoreType.DMA((2, blocks, members, 2)),
                pltpu.SemaphoreType.DMA((kb,)),
            ]),
        out_shape=[jax.ShapeDtypeStruct((4, steps, members // 4 * beams, width), jnp.bfloat16)] * 2,
        compiler_params=pltpu.CompilerParams(vmem_limit_bytes=40 * 2**20),
        cost_estimate=pl.CostEstimate(flops=int(steps * 2.8e9), bytes_accessed=steps * 7 * 2**20, transcendentals=0),
    )(pick, foot, table, pulses, weight, weight, bank)


def body(pulses, footprint, proj_weight, bank, merge_index):
    position = lax.axis_index("sub")
    width = bank.shape[1]
    owners, beams, _ = proj_weight.shape
    held = pulses[0]
    blocks = held.shape[2] // width
    levels = merge_index.shape[0]
    table = lax.dynamic_slice_in_dim(merge_index[:, 0], position * blocks, blocks, axis=2).reshape(-1)
    groups = lax.axis_size("grp")
    pick = jnp.repeat(jnp.arange(groups, dtype=jnp.int32), blocks)
    parts = images_of(held, footprint.reshape(-1), table, proj_weight, bank, pick, levels)
    cores = 8
    planes = owners // cores
    rows_of = [[start + i for i in range(cores)] for start in range(0, owners, cores)]
    lines_of = [[start + i * cores for i in range(planes)] for start in range(cores)]
    done = []
    for part in parts:
        summed = lax.psum_scatter(part, "grp", scatter_dimension=0, tiled=True)
        spread = lax.all_to_all(summed[0], "sub", 0, 0, axis_index_groups=lines_of, tiled=True)
        turned = lax.all_to_all(spread, "grp", 0, 0, tiled=True)
        by_owner = turned.reshape(groups, 2, beams, width).transpose(1, 0, 2, 3).reshape(cores, beams, width)
        done.append(lax.all_to_all(by_owner, "sub", 0, 0, axis_index_groups=rows_of, tiled=True))
    slab = jnp.stack(done, axis=2)
    return slab.transpose(1, 0, 2, 3).reshape(beams, cores * blocks * width)


def solution(mesh):
    placed = (P("grp", None, None, "sub"), P(), P(), P(), P(None, "grp", None, None, None))
    return jax.shard_map(
        body, mesh=mesh, in_specs=placed, out_specs=P("sub", "grp"), check_vma=False
    )
```

```python
import functools
import jax
import jax.numpy as jnp
from jax import lax
from jax.experimental import pallas as pl
from jax.experimental.pallas import tpu as pltpu
from jax.sharding import PartitionSpec as P

CHUNK = 4
ROUND = 12
LINE, CORES, TEAM, RING = 4, 2, 8, 4
VMEM = 56 * 2**20

f32, bf16, i32 = jnp.float32, jnp.bfloat16, jnp.int32
ANY = pl.BlockSpec(memory_space=pl.ANY)


def where_am_i():
    sub = lax.axis_index("sub")
    return lax.axis_index("grp"), sub >> 3, (sub >> 1) & 3, sub & 1


def run(copies):
    for c in copies:
        c.start()
    for c in copies:
        c.wait()


def row_fetches(block, pulses_ref, rows, row_sem):
    width = rows.shape[2]
    return [
        pltpu.make_async_copy(pulses_ref.at[j, :, pl.ds(block * width, width)], rows.at[j], row_sem.at[j])
        for j in range(rows.shape[0])
    ]


def project(foot, weights, rows, image):
    for o in range(weights.shape[0]):
        both = jnp.concatenate([rows[o], rows[foot[1, o]]], axis=0)
        image[o] = jnp.dot(weights[o], both, preferred_element_type=f32).astype(bf16)


def start_kernel(block, foot_ref, pulses_ref, weight_ref, *rest):
    outs, (foot, rows, weights, image, row_sem, sem, out_sem) = rest[:RING], rest[RING:]
    first = [pltpu.make_async_copy(foot_ref, foot, sem.at[0]), pltpu.make_async_copy(weight_ref, weights, sem.at[1])]
    copies = first + row_fetches(block, pulses_ref, rows, row_sem)
    run(copies)
    project(foot, weights, rows, image)
    _, z, _, _ = where_am_i()
    run([
        pltpu.make_async_copy(image.at[pl.ds(((z + d) & 3) * TEAM, TEAM)], outs[d], out_sem.at[d])
        for d in (1, 3, 2, 0)
    ])


def start_images(block, foot, pulses, weight, width):
    owners, beams, depth = weight.shape
    return pl.pallas_call(
        functools.partial(start_kernel, block),
        in_specs=[ANY] * 3,
        out_specs=[ANY] * RING,
        out_shape=[jax.ShapeDtypeStruct((TEAM, beams, width), bf16)] * RING,
        scratch_shapes=[
            pltpu.SMEM(foot.shape, i32),
            pltpu.VMEM((owners, depth // 2, width), bf16),
            pltpu.VMEM((owners, beams, depth), bf16),
            pltpu.VMEM((owners, beams, width), bf16),
            pltpu.SemaphoreType.DMA((owners,)),
            pltpu.SemaphoreType.DMA((2,)),
            pltpu.SemaphoreType.DMA((RING,)),
        ],
        compiler_params=pltpu.CompilerParams(vmem_limit_bytes=VMEM),
        cost_estimate=pl.CostEstimate(flops=400_000_000, bytes_accessed=7 * 2**20, transcendentals=0),
        name="start",
    )(foot, pulses, weight)


def tree_kernel(joined, block, levels, *refs):
    if joined:
        part_refs, (index_ref, bank_ref), refs = refs[:RING], refs[RING:RING + 2], refs[RING + 2:]
        outs, refs = refs[:5], refs[5:]
    else:
        (foot_ref, pulses_ref, weight_ref, _, index_ref, bank_ref), refs = refs[:6], refs[6:]
        outs, refs = refs[:RING], refs[RING:]
    index, mats, image, acc, stage, sem, row_sem, mat_sem, out_sem = refs[:9]
    lists, refs = refs[9:9 + 5 * 2 * levels], refs[9 + 5 * 2 * levels:]
    images, beams, width = stage.shape[0] - 1, stage.shape[1], stage.shape[2]
    kinds = mats.shape[0]
    passes = 2 * levels
    most = (images + kinds * (CHUNK - 1)) // CHUNK
    y, z, x, c = where_am_i()
    blocks = index.shape[3] // (RING * TEAM)

    index_copy = pltpu.make_async_copy(index_ref, index, sem.at[0])
    mat_copies = [pltpu.make_async_copy(bank_ref.at[k], mats.at[k], mat_sem.at[k]) for k in range(kinds)]
    if joined:
        feeds = [
            pltpu.make_async_copy(part_refs[d], image.at[0, pl.ds(d * TEAM, TEAM)], row_sem.at[d])
            for d in range(RING)
        ]
    else:
        foot, rows, weights = refs
        feeds = [
            pltpu.make_async_copy(foot_ref, foot, sem.at[1]),
            pltpu.make_async_copy(weight_ref, weights, sem.at[2]),
        ] + row_fetches(block, pulses_ref, rows, row_sem)
    for copy in [index_copy] + feeds + mat_copies:
        copy.start()

    def kind_of(p, i):
        if joined:
            owner = z * TEAM + i % TEAM
            column = (((z - i // TEAM) & 3) * TEAM + x * CORES + c) * blocks + block
        else:
            owner = i
            column = ((z * LINE + x) * CORES + c) * blocks + block
        return index[p // 2, owner, p % 2, column]

    def sort_pass(p):
        counts, starts, ranks, slots, entries = lists[5 * p:5 * p + 5]
        for k in range(kinds):
            counts[k] = 0
        for q in range(most):
            entries[q] = 0
            for i in range(CHUNK):
                slots[q * CHUNK + i] = images
        for i in range(images):
            k = kind_of(p, i)
            n = counts[k]
            ranks[i] = n
            counts[k] = n + 1
        begin = 0
        for k in range(kinds):
            starts[k] = begin * CHUNK
            begin = begin + ((counts[k] + (CHUNK - 1)) >> 2)
        for i in range(images):
            k = kind_of(p, i)
            place = starts[k] + ranks[i]
            slots[place] = i
            entries[place >> 2] = k
        return begin

    def chunk(p, q):
        level, which = p // 2, p % 2
        slots, entries = lists[5 * p + 3:5 * p + 5]
        now, later = level % 2, (level + 1) % 2
        dest = [slots[q * CHUNK + i] for i in range(CHUNK)]
        source = [d if which == 0 else jnp.bitwise_xor(d, 1 << level) for d in dest]
        many = jnp.concatenate([image[now, s] for s in source], axis=0)
        out = jnp.dot(many, mats[entries[q]], preferred_element_type=f32)
        for i, d in enumerate(dest):
            part = out[i * beams:(i + 1) * beams]
            if which == 0:
                acc[d] = part
            elif level + 1 < levels:
                image[later, d] = (acc[d] + part).astype(bf16)
            else:
                xo, co = (d >> 1) & 3, d & 1
                if joined:
                    place = ((((z - (d >> 3)) & 3) - y) & 3) * TEAM + ((xo - x) & 3) * CORES + co
                else:
                    place = ((xo - y) & 3) * TEAM + (((d >> 3) - z) & 3) * CORES + co
                stage[jnp.where(d == images, images, place)] = (acc[d] + part).astype(bf16)

    index_copy.wait()
    used = sort_pass(0)
    for copy in feeds:
        copy.wait()
    if not joined:
        project(foot, weights, rows, image.at[0])
    for copy in mat_copies:
        copy.wait()
    for p in range(passes):
        after = sort_pass(p + 1) if p + 1 < passes else None
        for q in range(ROUND):
            chunk(p, q)

        @pl.when(used > ROUND)
        def _(p=p):
            for q in range(ROUND, most):
                chunk(p, q)

        used = after

    half = TEAM // 2
    if joined:
        moves = [
            (2 * TEAM, half, outs[0].at[0]), (TEAM + half, half, outs[0].at[1]),
            (2 * TEAM + half, half, outs[1].at[0]), (3 * TEAM, half, outs[1].at[1]),
            (TEAM, half, outs[2]), (3 * TEAM + half, half, outs[3]), (0, TEAM, outs[4]),
        ]
    else:
        moves = [(r * TEAM, TEAM, outs[r]) for r in (2, 1, 3, 0)]
    run([
        pltpu.make_async_copy(stage.at[pl.ds(s, n)], ref, out_sem.at[i]) for i, (s, n, ref) in enumerate(moves)
    ])


def trees(joined, block, index, bank, beams, feeds):
    kinds, width, _ = bank.shape
    levels, images = index.shape[:2]
    most = (images + kinds * (CHUNK - 1)) // CHUNK
    whole = jax.ShapeDtypeStruct((TEAM, beams, width), bf16)
    pair = jax.ShapeDtypeStruct((2, TEAM // 2, beams, width), bf16)
    piece = jax.ShapeDtypeStruct((TEAM // 2, beams, width), bf16)
    scratch = [
        pltpu.SMEM(index.shape, i32),
        pltpu.VMEM(bank.shape, bf16),
        pltpu.VMEM((2, images + TEAM, beams, width), bf16),
        pltpu.VMEM((images + 1, beams, width), f32),
        pltpu.VMEM((images + 1, beams, width), bf16),
        pltpu.SemaphoreType.DMA((3,)),
        pltpu.SemaphoreType.DMA((images,)),
        pltpu.SemaphoreType.DMA((kinds,)),
        pltpu.SemaphoreType.DMA((7,)),
    ]
    for _ in range(2 * levels):
        scratch += [pltpu.SMEM((n,), i32) for n in (kinds, kinds, images, most * CHUNK, most)]
    if not joined:
        foot, pulses, weight, _ = feeds
        owners, _, depth = weight.shape
        scratch += [
            pltpu.SMEM(foot.shape, i32),
            pltpu.VMEM((owners, depth // 2, width), bf16),
            pltpu.VMEM((owners, beams, depth), bf16),
        ]
    out_shape = [pair, pair, piece, piece, whole] if joined else [whole] * RING
    return pl.pallas_call(
        functools.partial(tree_kernel, joined, block, levels),
        in_specs=[ANY] * (len(feeds) + 2),
        out_specs=[ANY] * len(out_shape),
        out_shape=out_shape,
        scratch_shapes=scratch,
        compiler_params=pltpu.CompilerParams(vmem_limit_bytes=VMEM),
        cost_estimate=pl.CostEstimate(flops=9_000_000_000, bytes_accessed=11 * 2**20, transcendentals=0),
        name="joined_trees" if joined else "trees",
    )(*feeds, index, bank)


def lay_kernel(*refs):
    mine, other, out_ref = refs[:-2], refs[-2], refs[-1]
    _, _, x, c = where_am_i()
    width = other.shape[2]
    blocks = len(mine) // LINE
    for b in range(blocks):
        for d in range(LINE):
            for part, core in ((mine[b * LINE + d][c], c), (other[b * LINE + d], 1 - c)):
                at = ((((x - d) & 3) * CORES + core) * blocks + b) * width
                out_ref[:, pl.ds(pl.multiple_of(at, width), width)] = part


def total(*parts):
    out = parts[0].astype(f32)
    for part in parts[1:]:
        out = out + part.astype(f32)
    return out.astype(bf16)


def turn(pieces, shift):
    return [lax.select_n((shift - d) & 3, *pieces) for d in range(len(pieces))]


def body(pulses, footprint, proj_weight, bank, merge_index):
    held = pulses[0]
    width = bank.shape[1]
    owners, beams, _ = proj_weight.shape
    y, z, x, c = where_am_i()
    foot = footprint.T
    index = merge_index[:, 0].transpose(0, 1, 3, 2)

    def along_y(value, d):
        return lax.ppermute(value, "grp", [(i, (i + d) % RING) for i in range(RING)])

    def along_sub(value, move):
        return lax.ppermute(value, "sub", [(i, move(i >> 3, (i >> 1) & 3, i & 1)) for i in range(owners)])

    def along_z(value, d):
        return along_sub(value, lambda zz, xx, cc: ((zz + d) % RING) * TEAM + xx * CORES + cc)

    def along_x(value, d):
        return along_sub(value, lambda zz, xx, cc: zz * TEAM + ((xx + d) % LINE) * CORES + cc)

    def exchange(pieces, along):
        return [pieces[0]] + [along(pieces[d], d) for d in range(1, len(pieces))]

    begun = start_images(0, foot, held, proj_weight, width)
    spread = exchange(begun, along_z)
    sent = trees(False, 1, index, bank, beams, (foot, held, proj_weight, begun[0]))
    got = exchange(sent, along_y)
    to_up, to_down, keep_up, keep_down, own = trees(True, 0, index, bank, beams, tuple(spread))
    got, own = lax.optimization_barrier((got, own))
    from_down, from_up = along_y(to_up, 1), along_y(to_down, -1)
    last_down = along_y(total(from_down[0], keep_up), 1)
    last_up = along_y(total(from_up[0], keep_down), -1)
    half = TEAM // 2

    summed = []
    for r in range(LINE):
        low = r * CORES < half
        lo = r * CORES - (0 if low else half)
        near, far = (last_down, from_up[1]) if low else (last_up, from_down[1])
        summed.append(total(own[r * CORES:(r + 1) * CORES], near[lo:lo + CORES], far[lo:lo + CORES]))
    first = exchange(summed, along_x)

    pieces = [total(*[g[r * CORES:(r + 1) * CORES] for g in got]) for r in range(RING)]
    pieces = exchange(pieces, along_z)
    pieces = exchange(turn(pieces, z - y), along_y)
    second = exchange(turn(pieces, y - x), along_x)
    mine = first + second
    other = jnp.stack([jnp.where(c == 0, piece[1], piece[0]) for piece in mine])
    other = along_sub(other, lambda zz, xx, cc: zz * TEAM + xx * CORES + 1 - cc)

    return pl.pallas_call(
        lay_kernel,
        out_shape=jax.ShapeDtypeStruct((beams, LINE * CORES * 2 * width), bf16),
        name="lay",
    )(*mine, other)


def solution(mesh):
    placed = (P("grp", None, None, "sub"), P(), P(), P(), P(None, "grp", None, None, None))
    return jax.shard_map(
        body, mesh=mesh, in_specs=placed, out_specs=P("sub", "grp"), check_vma=False
    )
```

```python
import functools
import jax
import jax.numpy as jnp
from jax import lax
from jax.experimental import pallas as pl
from jax.experimental.pallas import tpu as pltpu
from jax.sharding import PartitionSpec as P

TAKE = 10
MORE = 4
ROOM = 64
LINE, CORES, TEAM, RING = 4, 2, 8, 4
VMEM = 28 * 2**20
ALL_VMEM = 58 * 2**20

f32, bf16, i32 = jnp.float32, jnp.bfloat16, jnp.int32
ANY = pl.BlockSpec(memory_space=pl.ANY)
HBM = pl.BlockSpec(memory_space=pltpu.HBM)


def where_am_i():
    sub = lax.axis_index("sub")
    return lax.axis_index("grp"), sub >> 3, (sub >> 1) & 3, sub & 1


def run(copies):
    for c in copies:
        c.start()
    for c in copies:
        c.wait()


def row_fetches(block, pulses_ref, rows, row_sem):
    width = rows.shape[2]
    return [
        pltpu.make_async_copy(pulses_ref.at[j, :, pl.ds(block * width, width)], rows.at[j], row_sem.at[j])
        for j in range(rows.shape[0])
    ]


def projected(o, foot, weights, rows):
    both = jnp.concatenate([rows[o], rows[foot[1, o]]], axis=0)
    return jnp.dot(weights[o], both, preferred_element_type=f32).astype(bf16)


def start_kernel(block, foot_ref, pulses_ref, weight_ref, *rest):
    outs, (foot, rows, weights, image, row_sem, sem, out_sem) = rest[:RING], rest[RING:]
    first = [pltpu.make_async_copy(foot_ref, foot, sem.at[0]), pltpu.make_async_copy(weight_ref, weights, sem.at[1])]
    copies = first + row_fetches(block, pulses_ref, rows, row_sem)
    run(copies)
    _, z, _, _ = where_am_i()
    sends = []
    for d in (1, 3, 2, 0):
        for j in range(TEAM):
            o = ((z + d) & 3) * TEAM + j
            image[d * TEAM + j] = projected(o, foot, weights, rows)
        sends.append(pltpu.make_async_copy(image.at[pl.ds(d * TEAM, TEAM)], outs[d], out_sem.at[d]))
        sends[-1].start()
    for copy in sends:
        copy.wait()


def start_images(block, foot, pulses, weight, width):
    owners, beams, depth = weight.shape
    return pl.pallas_call(
        functools.partial(start_kernel, block),
        in_specs=[HBM] * 3,
        out_specs=[ANY] * RING,
        out_shape=[jax.ShapeDtypeStruct((TEAM, beams, width), bf16)] * RING,
        scratch_shapes=[
            pltpu.SMEM(foot.shape, i32),
            pltpu.VMEM((owners, depth // 2, width), bf16),
            pltpu.VMEM((owners, beams, depth), bf16),
            pltpu.VMEM((owners, beams, width), bf16),
            pltpu.SemaphoreType.DMA((owners,)),
            pltpu.SemaphoreType.DMA((2,)),
            pltpu.SemaphoreType.DMA((RING,)),
        ],
        compiler_params=pltpu.CompilerParams(vmem_limit_bytes=ALL_VMEM),
        cost_estimate=pl.CostEstimate(flops=400_000_000, bytes_accessed=7 * 2**20, transcendentals=0),
        name="start",
    )(foot, pulses, weight)


def tree_kernel(joined, block, levels, *refs):
    if joined:
        part_refs, (index_ref, bank_ref), refs = refs[:RING], refs[RING:RING + 2], refs[RING + 2:]
        outs, refs = refs[:5], refs[5:]
    else:
        (foot_ref, pulses_ref, weight_ref, _, index_ref, bank_ref), refs = refs[:6], refs[6:]
        outs, refs = refs[:RING], refs[RING:]
    index, mats, image, acc, stage, sem, row_sem, mat_sem, out_sem = refs[:9]
    lists, refs = refs[9:9 + 2 * levels], refs[9 + 2 * levels:]
    images, beams, width = stage.shape[0], stage.shape[1], stage.shape[2]
    kinds = mats.shape[0]
    y, z, x, c = where_am_i()
    blocks = index.shape[3] // (RING * TEAM)

    index_copy = pltpu.make_async_copy(index_ref, index, sem.at[0])
    mat_copies = [pltpu.make_async_copy(bank_ref.at[k], mats.at[k], mat_sem.at[k]) for k in range(kinds)]
    if joined:
        feeds = [
            pltpu.make_async_copy(part_refs[d], image.at[0, pl.ds(d * TEAM, TEAM)], row_sem.at[d])
            for d in range(RING)
        ]
    else:
        foot, rows, weights = refs
        feeds = [
            pltpu.make_async_copy(foot_ref, foot, sem.at[1]),
            pltpu.make_async_copy(weight_ref, weights, sem.at[2]),
        ] + row_fetches(block, pulses_ref, rows, row_sem)
    for copy in [index_copy] + feeds + mat_copies:
        copy.start()

    def kind_of(level, which, i):
        if joined:
            owner = z * TEAM + i % TEAM
            column = (((z - i // TEAM) & 3) * TEAM + x * CORES + c) * blocks + block
        else:
            owner = i
            column = ((z * LINE + x) * CORES + c) * blocks + block
        return index[level, owner, which, column]

    def sort_level(level):
        counts, uses = lists[2 * level:2 * level + 2]
        for k in range(kinds):
            counts[k] = 0
            for i in range(TAKE):
                uses[k * ROOM + i] = images
        for which in range(2):
            for i in range(images):
                k = kind_of(level, which, i)
                n = counts[k]
                uses[k * ROOM + n] = which * ROOM + i
                counts[k] = n + 1

    def multiply(level, k, taken):
        which = [v >> 6 for v in taken]
        dest = [v & (ROOM - 1) for v in taken]
        many = jnp.concatenate(
            [image[level % 2, jnp.bitwise_xor(d, w << level)] for d, w in zip(dest, which)], axis=0)
        out = jnp.dot(many, mats[k], preferred_element_type=f32)
        for i, (d, w) in enumerate(zip(dest, which)):
            acc[w, d] = out[i * beams:(i + 1) * beams]

    def merge(level):
        counts, uses = lists[2 * level:2 * level + 2]
        for k in range(kinds):
            if level == 0:
                mat_copies[k].wait()
            multiply(level, k, [uses[k * ROOM + i] for i in range(TAKE)])

        def rest(k, carry):
            n = counts[k]

            def more(t, carry):
                first = TAKE + t * MORE
                multiply(level, k, [
                    jnp.where(first + i < n, uses[k * ROOM + first + i], images) for i in range(MORE)])
                return carry

            return lax.fori_loop(0, (jnp.maximum(n - TAKE, 0) + (MORE - 1)) >> 2, more, carry)

        lax.fori_loop(0, kinds, rest, 0)
        for d in range(images):
            merged = (acc[0, d] + acc[1, d]).astype(bf16)
            if level + 1 < levels:
                image[(level + 1) % 2, d] = merged
            else:
                team, xo, co = d // TEAM, (d // CORES) % LINE, d % CORES
                if joined:
                    place = ((z - team - y) & 3) * TEAM + ((xo - x) & 3) * CORES + co
                else:
                    place = ((xo - y) & 3) * TEAM + ((team - z) & 3) * CORES + co
                stage[place] = merged

    index_copy.wait()
    sort_level(0)
    for copy in feeds:
        copy.wait()
    if not joined:
        for o in range(images):
            image[0, o] = projected(o, foot, weights, rows)
    for level in range(levels):
        if level + 1 < levels:
            sort_level(level + 1)
        merge(level)

    half = TEAM // 2
    if joined:
        moves = [
            (2 * TEAM, half, outs[0].at[0]), (TEAM + half, half, outs[0].at[1]),
            (2 * TEAM + half, half, outs[1].at[0]), (3 * TEAM, half, outs[1].at[1]),
            (TEAM, half, outs[2]), (3 * TEAM + half, half, outs[3]), (0, TEAM, outs[4]),
        ]
    else:
        moves = [(r * TEAM, TEAM, outs[r]) for r in (2, 1, 3, 0)]
    run([
        pltpu.make_async_copy(stage.at[pl.ds(s, n)], ref, out_sem.at[i]) for i, (s, n, ref) in enumerate(moves)
    ])


def trees(joined, block, index, bank, beams, feeds):
    kinds, width, _ = bank.shape
    levels, images = index.shape[:2]
    whole = jax.ShapeDtypeStruct((TEAM, beams, width), bf16)
    pair = jax.ShapeDtypeStruct((2, TEAM // 2, beams, width), bf16)
    piece = jax.ShapeDtypeStruct((TEAM // 2, beams, width), bf16)
    scratch = [
        pltpu.SMEM(index.shape, i32),
        pltpu.VMEM(bank.shape, bf16),
        pltpu.VMEM((2, images + TEAM, beams, width), bf16),
        pltpu.VMEM((2, images + 1, beams, width), f32),
        pltpu.VMEM((images, beams, width), bf16),
        pltpu.SemaphoreType.DMA((3,)),
        pltpu.SemaphoreType.DMA((images,)),
        pltpu.SemaphoreType.DMA((kinds,)),
        pltpu.SemaphoreType.DMA((7,)),
    ]
    for _ in range(levels):
        scratch += [pltpu.SMEM((n,), i32) for n in (kinds, kinds * ROOM + TAKE)]
    if not joined:
        foot, pulses, weight, _ = feeds
        owners, _, depth = weight.shape
        scratch += [
            pltpu.SMEM(foot.shape, i32),
            pltpu.VMEM((owners, depth // 2, width), bf16),
            pltpu.VMEM((owners, beams, depth), bf16),
        ]
    out_shape = [pair, pair, piece, piece, whole] if joined else [whole] * RING
    return pl.pallas_call(
        functools.partial(tree_kernel, joined, block, levels),
        in_specs=[ANY if joined else HBM] * len(feeds) + [HBM] * 2,
        out_specs=[ANY] * len(out_shape),
        out_shape=out_shape,
        scratch_shapes=scratch,
        compiler_params=pltpu.CompilerParams(vmem_limit_bytes=VMEM if joined else ALL_VMEM),
        cost_estimate=pl.CostEstimate(flops=9_000_000_000, bytes_accessed=11 * 2**20, transcendentals=0),
        name="joined_trees" if joined else "trees",
    )(*feeds, index, bank)


def lay_kernel(*refs):
    mine, (other, out_ref, slab, sem, out_sem) = refs[:LINE], refs[LINE:]
    _, _, x, c = where_am_i()
    _, blocks, _, width = other.shape
    copies = []
    for d in range(LINE):
        for b in range(blocks):
            for source, core in ((mine[d].at[b, c], c), (other.at[d, b], 1 - c)):
                at = ((((x - d) & 3) * CORES + core) * blocks + b) * width
                copies.append(pltpu.make_async_copy(
                    source, slab.at[:, pl.ds(pl.multiple_of(at, width), width)], sem.at[len(copies)]))
    run(copies)
    run([pltpu.make_async_copy(slab, out_ref, out_sem)])


def total(*parts):
    out = parts[0].astype(f32)
    for part in parts[1:]:
        out = out + part.astype(f32)
    return out.astype(bf16)


def turn(pieces, shift):
    return [lax.select_n((shift - d) & 3, *pieces) for d in range(len(pieces))]


def body(pulses, footprint, proj_weight, bank, merge_index):
    held = pulses[0]
    width = bank.shape[1]
    owners, beams, _ = proj_weight.shape
    y, z, x, c = where_am_i()
    foot = footprint.T
    index = merge_index[:, 0].transpose(0, 1, 3, 2)
    held, foot, proj_weight, bank, index = [
        pltpu.with_memory_space_constraint(a, pltpu.HBM) for a in (held, foot, proj_weight, bank, index)
    ]

    def along_y(value, d):
        return lax.ppermute(value, "grp", [(i, (i + d) % RING) for i in range(RING)])

    def along_sub(value, move):
        return lax.ppermute(value, "sub", [(i, move(i >> 3, (i >> 1) & 3, i & 1)) for i in range(owners)])

    def along_z(value, d):
        return along_sub(value, lambda zz, xx, cc: ((zz + d) % RING) * TEAM + xx * CORES + cc)

    def along_x(value, d):
        return along_sub(value, lambda zz, xx, cc: zz * TEAM + ((xx + d) % LINE) * CORES + cc)

    def exchange(pieces, along):
        return [pieces[0]] + [along(pieces[d], d) for d in range(1, len(pieces))]

    begun = start_images(0, foot, held, proj_weight, width)
    spread = exchange(begun, along_z)
    sent = trees(False, 1, index, bank, beams, (foot, held, proj_weight, begun[0]))
    got = exchange(sent, along_y)
    to_up, to_down, keep_up, keep_down, own = trees(True, 0, index, bank, beams, tuple(spread))
    got, own = lax.optimization_barrier((got, own))
    from_down, from_up = along_y(to_up, 1), along_y(to_down, -1)
    pieces = [total(*[g[r * CORES:(r + 1) * CORES] for g in got]) for r in range(RING)]
    pieces = exchange(pieces, along_z)
    from_down, from_up, pieces = lax.optimization_barrier((from_down, from_up, pieces))
    last_down = along_y(total(from_down[0], keep_up), 1)
    last_up = along_y(total(from_up[0], keep_down), -1)
    pieces = exchange(turn(pieces, z - y), along_y)
    last_down, last_up, pieces = lax.optimization_barrier((last_down, last_up, pieces))
    half = TEAM // 2

    summed = []
    for r in range(LINE):
        low = r * CORES < half
        lo = r * CORES - (0 if low else half)
        near, far = (last_down, from_up[1]) if low else (last_up, from_down[1])
        summed.append(total(own[r * CORES:(r + 1) * CORES], near[lo:lo + CORES], far[lo:lo + CORES]))

    mine = exchange([jnp.stack(both) for both in zip(summed, turn(pieces, y - x))], along_x)
    other = jnp.stack([jnp.where(c == 0, piece[:, 1], piece[:, 0]) for piece in mine])
    other = along_sub(other, lambda zz, xx, cc: zz * TEAM + xx * CORES + 1 - cc)

    return pl.pallas_call(
        lay_kernel,
        in_specs=[ANY] * (LINE + 1),
        out_specs=ANY,
        out_shape=jax.ShapeDtypeStruct((beams, LINE * CORES * 2 * width), bf16),
        scratch_shapes=[
            pltpu.VMEM((beams, LINE * CORES * 2 * width), bf16),
            pltpu.SemaphoreType.DMA((2 * CORES * LINE,)),
            pltpu.SemaphoreType.DMA,
        ],
        compiler_params=pltpu.CompilerParams(vmem_limit_bytes=4 * 2**20),
        name="lay",
    )(*mine, other)


def solution(mesh):
    placed = (P("grp", None, None, "sub"), P(), P(), P(), P(None, "grp", None, None, None))
    return jax.shard_map(
        body, mesh=mesh, in_specs=placed, out_specs=P("sub", "grp"), check_vma=False
    )
```

```python
import functools
import jax
import jax.numpy as jnp
from jax import lax
from jax.experimental import pallas as pl
from jax.experimental.pallas import tpu as pltpu
from jax.sharding import PartitionSpec as P

TAKE = 10
MORE = 4
ROOM = 64
LINE, CORES, TEAM, RING = 4, 2, 8, 4
VMEM = 28 * 2**20
ALL_VMEM = 28 * 2**20

f32, bf16, i32 = jnp.float32, jnp.bfloat16, jnp.int32
ANY = pl.BlockSpec(memory_space=pl.ANY)
HBM = pl.BlockSpec(memory_space=pltpu.HBM)


def where_am_i():
    sub = lax.axis_index("sub")
    return lax.axis_index("grp"), sub >> 3, (sub >> 1) & 3, sub & 1


def run(copies):
    for c in copies:
        c.start()
    for c in copies:
        c.wait()


def row_fetches(block, pulses_ref, rows, row_sem):
    width = rows.shape[2]
    return [
        pltpu.make_async_copy(pulses_ref.at[j, :, pl.ds(block * width, width)], rows.at[j], row_sem.at[j])
        for j in range(rows.shape[0])
    ]


def projected(o, foot, weights, rows):
    both = jnp.concatenate([rows[o], rows[foot[1, o]]], axis=0)
    return jnp.dot(weights[o], both, preferred_element_type=f32).astype(bf16)


def start_kernel(block, foot_ref, pulses_ref, weight_ref, *rest):
    outs, (foot, rows, weights, image, row_sem, sem, out_sem) = rest[:RING], rest[RING:]
    first = [pltpu.make_async_copy(foot_ref, foot, sem.at[0]), pltpu.make_async_copy(weight_ref, weights, sem.at[1])]
    copies = first + row_fetches(block, pulses_ref, rows, row_sem)
    run(copies)
    _, z, _, _ = where_am_i()
    sends = []
    for d in (1, 3, 2, 0):
        for j in range(TEAM):
            o = ((z + d) & 3) * TEAM + j
            image[d * TEAM + j] = projected(o, foot, weights, rows)
        sends.append(pltpu.make_async_copy(image.at[pl.ds(d * TEAM, TEAM)], outs[d], out_sem.at[d]))
        sends[-1].start()
    for copy in sends:
        copy.wait()


def start_images(block, foot, pulses, weight, width):
    owners, beams, depth = weight.shape
    return pl.pallas_call(
        functools.partial(start_kernel, block),
        in_specs=[HBM] * 3,
        out_specs=[ANY] * RING,
        out_shape=[jax.ShapeDtypeStruct((TEAM, beams, width), bf16)] * RING,
        scratch_shapes=[
            pltpu.SMEM(foot.shape, i32),
            pltpu.VMEM((owners, depth // 2, width), bf16),
            pltpu.VMEM((owners, beams, depth), bf16),
            pltpu.VMEM((owners, beams, width), bf16),
            pltpu.SemaphoreType.DMA((owners,)),
            pltpu.SemaphoreType.DMA((2,)),
            pltpu.SemaphoreType.DMA((RING,)),
        ],
        compiler_params=pltpu.CompilerParams(vmem_limit_bytes=ALL_VMEM),
        cost_estimate=pl.CostEstimate(flops=400_000_000, bytes_accessed=7 * 2**20, transcendentals=0),
        name="start",
    )(foot, pulses, weight)


def tree_kernel(joined, block, levels, *refs):
    if joined:
        part_refs, (index_ref, bank_ref), refs = refs[:RING], refs[RING:RING + 2], refs[RING + 2:]
        outs, refs = refs[:5], refs[5:]
    else:
        (foot_ref, pulses_ref, weight_ref, _, index_ref, bank_ref), refs = refs[:6], refs[6:]
        outs, refs = refs[:RING], refs[RING:]
    index, mats, image, acc, stage, sem, row_sem, mat_sem, out_sem = refs[:9]
    lists, refs = refs[9:9 + 2 * levels], refs[9 + 2 * levels:]
    images, beams, width = stage.shape[0], stage.shape[1], stage.shape[2]
    kinds = mats.shape[0]
    y, z, x, c = where_am_i()
    blocks = index.shape[3] // (RING * TEAM)

    index_copy = pltpu.make_async_copy(index_ref, index, sem.at[0])
    mat_copies = [pltpu.make_async_copy(bank_ref.at[k], mats.at[k], mat_sem.at[k]) for k in range(kinds)]
    if joined:
        feeds = [
            pltpu.make_async_copy(part_refs[d], image.at[0, pl.ds(d * TEAM, TEAM)], row_sem.at[d])
            for d in range(RING)
        ]
    else:
        foot, rows, weights = refs
        feeds = [
            pltpu.make_async_copy(foot_ref, foot, sem.at[1]),
            pltpu.make_async_copy(weight_ref, weights, sem.at[2]),
        ] + row_fetches(block, pulses_ref, rows, row_sem)
    for copy in [index_copy] + feeds + mat_copies:
        copy.start()

    def kind_of(level, which, i):
        if joined:
            owner = z * TEAM + i % TEAM
            column = (((z - i // TEAM) & 3) * TEAM + x * CORES + c) * blocks + block
        else:
            owner = i
            column = ((z * LINE + x) * CORES + c) * blocks + block
        return index[level, owner, which, column]

    def sort_level(level):
        counts, uses = lists[2 * level:2 * level + 2]
        for k in range(kinds):
            counts[k] = 0
            for i in range(TAKE):
                uses[k * ROOM + i] = images
        for which in range(2):
            for i in range(images):
                k = kind_of(level, which, i)
                n = counts[k]
                uses[k * ROOM + n] = which * ROOM + i
                counts[k] = n + 1

    def multiply(level, k, taken):
        which = [v >> 6 for v in taken]
        dest = [v & (ROOM - 1) for v in taken]
        many = jnp.concatenate(
            [image[level % 2, jnp.bitwise_xor(d, w << level)] for d, w in zip(dest, which)], axis=0)
        out = jnp.dot(many, mats[k], preferred_element_type=f32)
        for i, (d, w) in enumerate(zip(dest, which)):
            acc[w, d] = out[i * beams:(i + 1) * beams]

    def merge(level):
        counts, uses = lists[2 * level:2 * level + 2]
        for k in range(kinds):
            multiply(level, k, [uses[k * ROOM + i] for i in range(TAKE)])

        def rest(k, carry):
            n = counts[k]

            def more(t, carry):
                first = TAKE + t * MORE
                multiply(level, k, [
                    jnp.where(first + i < n, uses[k * ROOM + first + i], images) for i in range(MORE)])
                return carry

            return lax.fori_loop(0, (jnp.maximum(n - TAKE, 0) + (MORE - 1)) >> 2, more, carry)

        lax.fori_loop(0, kinds, rest, 0)
        for d in range(images):
            merged = (acc[0, d] + acc[1, d]).astype(bf16)
            if level + 1 < levels:
                image[(level + 1) % 2, d] = merged
            else:
                team, xo, co = d // TEAM, (d // CORES) % LINE, d % CORES
                if joined:
                    place = ((z - team - y) & 3) * TEAM + ((xo - x) & 3) * CORES + co
                else:
                    place = ((xo - y) & 3) * TEAM + ((team - z) & 3) * CORES + co
                stage[place] = merged

    index_copy.wait()
    for level in range(levels if joined else 1):
        sort_level(level)
    for copy in feeds:
        copy.wait()
    if not joined:
        for o in range(images):
            image[0, o] = projected(o, foot, weights, rows)
    for copy in mat_copies:
        copy.wait()
    for level in range(levels):
        if level + 1 < levels and not joined:
            sort_level(level + 1)
        merge(level)

    half = TEAM // 2
    if joined:
        moves = [
            (2 * TEAM, half, outs[0].at[0]), (TEAM + half, half, outs[0].at[1]),
            (2 * TEAM + half, half, outs[1].at[0]), (3 * TEAM, half, outs[1].at[1]),
            (TEAM, half, outs[2]), (3 * TEAM + half, half, outs[3]), (0, TEAM, outs[4]),
        ]
    else:
        moves = [(r * TEAM, TEAM, outs[r]) for r in (2, 1, 3, 0)]
    run([
        pltpu.make_async_copy(stage.at[pl.ds(s, n)], ref, out_sem.at[i]) for i, (s, n, ref) in enumerate(moves)
    ])


def trees(joined, block, index, bank, beams, feeds):
    kinds, width, _ = bank.shape
    levels, images = index.shape[:2]
    whole = jax.ShapeDtypeStruct((TEAM, beams, width), bf16)
    pair = jax.ShapeDtypeStruct((2, TEAM // 2, beams, width), bf16)
    piece = jax.ShapeDtypeStruct((TEAM // 2, beams, width), bf16)
    scratch = [
        pltpu.SMEM(index.shape, i32),
        pltpu.VMEM(bank.shape, bf16),
        pltpu.VMEM((2, images + TEAM, beams, width), bf16),
        pltpu.VMEM((2, images + 1, beams, width), f32),
        pltpu.VMEM((images, beams, width), bf16),
        pltpu.SemaphoreType.DMA((3,)),
        pltpu.SemaphoreType.DMA((images,)),
        pltpu.SemaphoreType.DMA((kinds,)),
        pltpu.SemaphoreType.DMA((7,)),
    ]
    for _ in range(levels):
        scratch += [pltpu.SMEM((n,), i32) for n in (kinds, kinds * ROOM + TAKE)]
    if not joined:
        foot, pulses, weight, _ = feeds
        owners, _, depth = weight.shape
        scratch += [
            pltpu.SMEM(foot.shape, i32),
            pltpu.VMEM((owners, depth // 2, width), bf16),
            pltpu.VMEM((owners, beams, depth), bf16),
        ]
    out_shape = [pair, pair, piece, piece, whole] if joined else [whole] * RING
    return pl.pallas_call(
        functools.partial(tree_kernel, joined, block, levels),
        in_specs=[ANY if joined else HBM] * len(feeds) + [HBM] * 2,
        out_specs=[ANY] * len(out_shape),
        out_shape=out_shape,
        scratch_shapes=scratch,
        compiler_params=pltpu.CompilerParams(vmem_limit_bytes=VMEM if joined else ALL_VMEM),
        cost_estimate=pl.CostEstimate(flops=9_000_000_000, bytes_accessed=11 * 2**20, transcendentals=0),
        name="joined_trees" if joined else "trees",
    )(*feeds, index, bank)


def lay_kernel(*refs):
    mine, (other, out_ref, slab, sem, out_sem) = refs[:LINE], refs[LINE:]
    _, _, x, c = where_am_i()
    _, blocks, _, width = other.shape
    copies = []
    for d in range(LINE):
        for b in range(blocks):
            for source, core in ((mine[d].at[b, c], c), (other.at[d, b], 1 - c)):
                at = ((((x - d) & 3) * CORES + core) * blocks + b) * width
                copies.append(pltpu.make_async_copy(
                    source, slab.at[:, pl.ds(pl.multiple_of(at, width), width)], sem.at[len(copies)]))
    run(copies)
    run([pltpu.make_async_copy(slab, out_ref, out_sem)])


def total(*parts):
    out = parts[0].astype(f32)
    for part in parts[1:]:
        out = out + part.astype(f32)
    return out.astype(bf16)


def turn(pieces, shift):
    return [lax.select_n((shift - d) & 3, *pieces) for d in range(len(pieces))]


def body(pulses, footprint, proj_weight, bank, merge_index):
    held = pulses[0]
    width = bank.shape[1]
    owners, beams, _ = proj_weight.shape
    y, z, x, c = where_am_i()
    foot = footprint.T
    index = merge_index[:, 0].transpose(0, 1, 3, 2)
    held, foot, proj_weight, bank, index = [
        pltpu.with_memory_space_constraint(a, pltpu.HBM) for a in (held, foot, proj_weight, bank, index)
    ]

    def along_y(value, d):
        return lax.ppermute(value, "grp", [(i, (i + d) % RING) for i in range(RING)])

    def along_sub(value, move):
        return lax.ppermute(value, "sub", [(i, move(i >> 3, (i >> 1) & 3, i & 1)) for i in range(owners)])

    def along_z(value, d):
        return along_sub(value, lambda zz, xx, cc: ((zz + d) % RING) * TEAM + xx * CORES + cc)

    def along_x(value, d):
        return along_sub(value, lambda zz, xx, cc: zz * TEAM + ((xx + d) % LINE) * CORES + cc)

    def exchange(pieces, along):
        return [pieces[0]] + [along(pieces[d], d) for d in range(1, len(pieces))]

    begun = start_images(0, foot, held, proj_weight, width)
    spread = exchange(begun, along_z)
    sent = trees(False, 1, index, bank, beams, (foot, held, proj_weight, begun[0]))
    got = exchange(sent, along_y)
    to_up, to_down, keep_up, keep_down, own = trees(True, 0, index, bank, beams, tuple(spread))
    got, own = lax.optimization_barrier((got, own))
    from_down, from_up = along_y(to_up, 1), along_y(to_down, -1)
    pieces = [total(*[g[r * CORES:(r + 1) * CORES] for g in got]) for r in range(RING)]
    pieces = exchange(pieces, along_z)
    from_down, from_up, pieces = lax.optimization_barrier((from_down, from_up, pieces))
    last_down = along_y(total(from_down[0], keep_up), 1)
    last_up = along_y(total(from_up[0], keep_down), -1)
    pieces = exchange(turn(pieces, z - y), along_y)
    last_down, last_up, pieces = lax.optimization_barrier((last_down, last_up, pieces))
    half = TEAM // 2

    summed = []
    for r in range(LINE):
        low = r * CORES < half
        lo = r * CORES - (0 if low else half)
        near, far = (last_down, from_up[1]) if low else (last_up, from_down[1])
        summed.append(total(own[r * CORES:(r + 1) * CORES], near[lo:lo + CORES], far[lo:lo + CORES]))

    mine = exchange([jnp.stack(both) for both in zip(summed, turn(pieces, y - x))], along_x)
    other = jnp.stack([jnp.where(c == 0, piece[:, 1], piece[:, 0]) for piece in mine])
    other = along_sub(other, lambda zz, xx, cc: zz * TEAM + xx * CORES + 1 - cc)

    return pl.pallas_call(
        lay_kernel,
        in_specs=[ANY] * (LINE + 1),
        out_specs=ANY,
        out_shape=jax.ShapeDtypeStruct((beams, LINE * CORES * 2 * width), bf16),
        scratch_shapes=[
            pltpu.VMEM((beams, LINE * CORES * 2 * width), bf16),
            pltpu.SemaphoreType.DMA((2 * CORES * LINE,)),
            pltpu.SemaphoreType.DMA,
        ],
        compiler_params=pltpu.CompilerParams(vmem_limit_bytes=4 * 2**20),
        name="lay",
    )(*mine, other)


def solution(mesh):
    placed = (P("grp", None, None, "sub"), P(), P(), P(), P(None, "grp", None, None, None))
    return jax.shard_map(
        body, mesh=mesh, in_specs=placed, out_specs=P("sub", "grp"), check_vma=False
    )
```

```python
import functools
import jax
import jax.numpy as jnp
from jax import lax
from jax.experimental import pallas as pl
from jax.experimental.pallas import tpu as pltpu
from jax.sharding import PartitionSpec as P

TAKE = 10
MORE = 4
ROOM = 64
LINE, CORES, TEAM, RING = 4, 2, 8, 4
VMEM = 28 * 2**20
ALL_VMEM = 28 * 2**20

f32, bf16, i32 = jnp.float32, jnp.bfloat16, jnp.int32
ANY = pl.BlockSpec(memory_space=pl.ANY)
HBM = pl.BlockSpec(memory_space=pltpu.HBM)


def where_am_i():
    sub = lax.axis_index("sub")
    return lax.axis_index("grp"), sub >> 3, (sub >> 1) & 3, sub & 1


def run(copies):
    for c in copies:
        c.start()
    for c in copies:
        c.wait()


def row_fetches(block, pulses_ref, rows, row_sem):
    width = rows.shape[2]
    return [
        pltpu.make_async_copy(
            pulses_ref.at[pl.ds(j, TEAM), :, pl.ds(block * width, width)], rows.at[pl.ds(j, TEAM)], row_sem.at[j])
        for j in range(0, rows.shape[0], TEAM)
    ]


def projected(o, foot, weights, rows):
    both = jnp.concatenate([rows[o], rows[foot[1, o]]], axis=0)
    return jnp.dot(weights[o], both, preferred_element_type=f32).astype(bf16)


def start_kernel(block, foot_ref, pulses_ref, weight_ref, *rest):
    outs, (foot, rows, weights, image, row_sem, sem, out_sem) = rest[:RING], rest[RING:]
    first = [pltpu.make_async_copy(foot_ref, foot, sem.at[0]), pltpu.make_async_copy(weight_ref, weights, sem.at[1])]
    copies = first + row_fetches(block, pulses_ref, rows, row_sem)
    run(copies)
    _, z, _, _ = where_am_i()
    sends = []
    for d in (1, 3, 2, 0):
        for j in range(TEAM):
            o = ((z + d) & 3) * TEAM + j
            image[d * TEAM + j] = projected(o, foot, weights, rows)
        sends.append(pltpu.make_async_copy(image.at[pl.ds(d * TEAM, TEAM)], outs[d], out_sem.at[d]))
        sends[-1].start()
    for copy in sends:
        copy.wait()


def start_images(block, foot, pulses, weight, width):
    owners, beams, depth = weight.shape
    return pl.pallas_call(
        functools.partial(start_kernel, block),
        in_specs=[HBM] * 3,
        out_specs=[ANY] * RING,
        out_shape=[jax.ShapeDtypeStruct((TEAM, beams, width), bf16)] * RING,
        scratch_shapes=[
            pltpu.SMEM(foot.shape, i32),
            pltpu.VMEM((owners, depth // 2, width), bf16),
            pltpu.VMEM((owners, beams, depth), bf16),
            pltpu.VMEM((owners, beams, width), bf16),
            pltpu.SemaphoreType.DMA((owners,)),
            pltpu.SemaphoreType.DMA((2,)),
            pltpu.SemaphoreType.DMA((RING,)),
        ],
        compiler_params=pltpu.CompilerParams(vmem_limit_bytes=ALL_VMEM),
        cost_estimate=pl.CostEstimate(flops=400_000_000, bytes_accessed=7 * 2**20, transcendentals=0),
        name="start",
    )(foot, pulses, weight)


def tree_kernel(joined, block, levels, *refs):
    if joined:
        part_refs, (index_ref, bank_ref), refs = refs[:RING], refs[RING:RING + 2], refs[RING + 2:]
        outs, refs = refs[:5], refs[5:]
    else:
        (foot_ref, pulses_ref, weight_ref, _, index_ref, bank_ref), refs = refs[:6], refs[6:]
        outs, refs = refs[:RING], refs[RING:]
    index, mats, image, acc, stage, sem, row_sem, mat_sem, out_sem = refs[:9]
    lists, refs = refs[9:9 + 2 * levels], refs[9 + 2 * levels:]
    images, beams, width = stage.shape[0], stage.shape[1], stage.shape[2]
    kinds = mats.shape[0]
    y, z, x, c = where_am_i()
    blocks = index.shape[3] // (RING * TEAM)

    index_copy = pltpu.make_async_copy(index_ref, index, sem.at[0])
    mat_copies = [
        pltpu.make_async_copy(bank_ref.at[pl.ds(k, 4)], mats.at[pl.ds(k, 4)], mat_sem.at[k])
        for k in range(0, kinds, 4)
    ]
    if joined:
        feeds = [
            pltpu.make_async_copy(part_refs[d], image.at[0, pl.ds(d * TEAM, TEAM)], row_sem.at[d])
            for d in range(RING)
        ]
    else:
        foot, rows, weights = refs
        feeds = [
            pltpu.make_async_copy(foot_ref, foot, sem.at[1]),
            pltpu.make_async_copy(weight_ref, weights, sem.at[2]),
        ] + row_fetches(block, pulses_ref, rows, row_sem)
    for copy in [index_copy] + feeds + mat_copies:
        copy.start()

    def kind_of(level, which, i):
        if joined:
            owner = z * TEAM + i % TEAM
            column = (((z - i // TEAM) & 3) * TEAM + x * CORES + c) * blocks + block
        else:
            owner = i
            column = ((z * LINE + x) * CORES + c) * blocks + block
        return index[level, owner, which, column]

    def sort_level(level):
        counts, uses = lists[2 * level:2 * level + 2]
        for k in range(kinds):
            counts[k] = 0
            for i in range(TAKE):
                uses[k * ROOM + i] = images
        for which in range(2):
            for i in range(images):
                k = kind_of(level, which, i)
                n = counts[k]
                uses[k * ROOM + n] = which * ROOM + i
                counts[k] = n + 1

    def multiply(level, k, taken):
        which = [v >> 6 for v in taken]
        dest = [v & (ROOM - 1) for v in taken]
        many = jnp.concatenate(
            [image[level % 2, jnp.bitwise_xor(d, w << level)] for d, w in zip(dest, which)], axis=0)
        out = jnp.dot(many, mats[k], preferred_element_type=f32)
        for i, (d, w) in enumerate(zip(dest, which)):
            acc[w, d] = out[i * beams:(i + 1) * beams]

    def merge(level):
        counts, uses = lists[2 * level:2 * level + 2]
        for k in range(kinds):
            multiply(level, k, [uses[k * ROOM + i] for i in range(TAKE)])

        def rest(k, carry):
            n = counts[k]

            def more(t, carry):
                first = TAKE + t * MORE
                multiply(level, k, [
                    jnp.where(first + i < n, uses[k * ROOM + first + i], images) for i in range(MORE)])
                return carry

            return lax.fori_loop(0, (jnp.maximum(n - TAKE, 0) + (MORE - 1)) >> 2, more, carry)

        lax.fori_loop(0, kinds, rest, 0)
        for d in range(images):
            merged = (acc[0, d] + acc[1, d]).astype(bf16)
            if level + 1 < levels:
                image[(level + 1) % 2, d] = merged
            else:
                team, xo, co = d // TEAM, (d // CORES) % LINE, d % CORES
                if joined:
                    place = ((z - team - y) & 3) * TEAM + ((xo - x) & 3) * CORES + co
                else:
                    place = ((xo - y) & 3) * TEAM + ((team - z) & 3) * CORES + co
                stage[place] = merged

    index_copy.wait()
    for level in range(levels):
        sort_level(level)
    for copy in feeds:
        copy.wait()
    if not joined:
        for o in range(images):
            image[0, o] = projected(o, foot, weights, rows)
    for copy in mat_copies:
        copy.wait()
    for level in range(levels):
        merge(level)

    half = TEAM // 2
    if joined:
        moves = [
            (2 * TEAM, half, outs[0].at[0]), (TEAM + half, half, outs[0].at[1]),
            (2 * TEAM + half, half, outs[1].at[0]), (3 * TEAM, half, outs[1].at[1]),
            (TEAM, half, outs[2]), (3 * TEAM + half, half, outs[3]), (0, TEAM, outs[4]),
        ]
    else:
        moves = [(r * TEAM, TEAM, outs[r]) for r in (2, 1, 3, 0)]
    run([
        pltpu.make_async_copy(stage.at[pl.ds(s, n)], ref, out_sem.at[i]) for i, (s, n, ref) in enumerate(moves)
    ])


def trees(joined, block, index, bank, beams, feeds):
    kinds, width, _ = bank.shape
    levels, images = index.shape[:2]
    whole = jax.ShapeDtypeStruct((TEAM, beams, width), bf16)
    pair = jax.ShapeDtypeStruct((2, TEAM // 2, beams, width), bf16)
    piece = jax.ShapeDtypeStruct((TEAM // 2, beams, width), bf16)
    scratch = [
        pltpu.SMEM(index.shape, i32),
        pltpu.VMEM(bank.shape, bf16),
        pltpu.VMEM((2, images + TEAM, beams, width), bf16),
        pltpu.VMEM((2, images + 1, beams, width), f32),
        pltpu.VMEM((images, beams, width), bf16),
        pltpu.SemaphoreType.DMA((3,)),
        pltpu.SemaphoreType.DMA((images,)),
        pltpu.SemaphoreType.DMA((kinds,)),
        pltpu.SemaphoreType.DMA((7,)),
    ]
    for _ in range(levels):
        scratch += [pltpu.SMEM((n,), i32) for n in (kinds, kinds * ROOM + TAKE)]
    if not joined:
        foot, pulses, weight, _ = feeds
        owners, _, depth = weight.shape
        scratch += [
            pltpu.SMEM(foot.shape, i32),
            pltpu.VMEM((owners, depth // 2, width), bf16),
            pltpu.VMEM((owners, beams, depth), bf16),
        ]
    out_shape = [pair, pair, piece, piece, whole] if joined else [whole] * RING
    return pl.pallas_call(
        functools.partial(tree_kernel, joined, block, levels),
        in_specs=[ANY if joined else HBM] * len(feeds) + [HBM] * 2,
        out_specs=[ANY] * len(out_shape),
        out_shape=out_shape,
        scratch_shapes=scratch,
        compiler_params=pltpu.CompilerParams(vmem_limit_bytes=VMEM if joined else ALL_VMEM),
        cost_estimate=pl.CostEstimate(flops=9_000_000_000, bytes_accessed=11 * 2**20, transcendentals=0),
        name="joined_trees" if joined else "trees",
    )(*feeds, index, bank)


def lay_kernel(*refs):
    mine, (other, out_ref, slab, sem, out_sem) = refs[:LINE], refs[LINE:]
    _, _, x, c = where_am_i()
    _, blocks, _, width = other.shape
    copies = []
    for d in range(LINE):
        for b in range(blocks):
            for source, core in ((mine[d].at[b, c], c), (other.at[d, b], 1 - c)):
                at = ((((x - d) & 3) * CORES + core) * blocks + b) * width
                copies.append(pltpu.make_async_copy(
                    source, slab.at[:, pl.ds(pl.multiple_of(at, width), width)], sem.at[len(copies)]))
    run(copies)
    run([pltpu.make_async_copy(slab, out_ref, out_sem)])


def total(*parts):
    out = parts[0].astype(f32)
    for part in parts[1:]:
        out = out + part.astype(f32)
    return out.astype(bf16)


def turn(pieces, shift):
    return [lax.select_n((shift - d) & 3, *pieces) for d in range(len(pieces))]


def body(pulses, footprint, proj_weight, bank, merge_index):
    held = pulses[0]
    width = bank.shape[1]
    owners, beams, _ = proj_weight.shape
    y, z, x, c = where_am_i()
    foot = footprint.T
    index = merge_index[:, 0].transpose(0, 1, 3, 2)
    held, foot, proj_weight, bank, index = [
        pltpu.with_memory_space_constraint(a, pltpu.HBM) for a in (held, foot, proj_weight, bank, index)
    ]

    def along_y(value, d):
        return lax.ppermute(value, "grp", [(i, (i + d) % RING) for i in range(RING)])

    def along_sub(value, move):
        return lax.ppermute(value, "sub", [(i, move(i >> 3, (i >> 1) & 3, i & 1)) for i in range(owners)])

    def along_z(value, d):
        return along_sub(value, lambda zz, xx, cc: ((zz + d) % RING) * TEAM + xx * CORES + cc)

    def along_x(value, d):
        return along_sub(value, lambda zz, xx, cc: zz * TEAM + ((xx + d) % LINE) * CORES + cc)

    def exchange(pieces, along):
        return [pieces[0]] + [along(pieces[d], d) for d in range(1, len(pieces))]

    begun = start_images(0, foot, held, proj_weight, width)
    spread = exchange(begun, along_z)
    sent = trees(False, 1, index, bank, beams, (foot, held, proj_weight, begun[0]))
    got = exchange(sent, along_y)
    to_up, to_down, keep_up, keep_down, own = trees(True, 0, index, bank, beams, tuple(spread))
    got, own = lax.optimization_barrier((got, own))
    from_down, from_up = along_y(to_up, 1), along_y(to_down, -1)
    pieces = [total(*[g[r * CORES:(r + 1) * CORES] for g in got]) for r in range(RING)]
    pieces = exchange(pieces, along_z)
    from_down, from_up, pieces = lax.optimization_barrier((from_down, from_up, pieces))
    last_down = along_y(total(from_down[0], keep_up), 1)
    last_up = along_y(total(from_up[0], keep_down), -1)
    pieces = exchange(turn(pieces, z - y), along_y)
    last_down, last_up, pieces = lax.optimization_barrier((last_down, last_up, pieces))
    half = TEAM // 2

    summed = []
    for r in range(LINE):
        low = r * CORES < half
        lo = r * CORES - (0 if low else half)
        near, far = (last_down, from_up[1]) if low else (last_up, from_down[1])
        summed.append(total(own[r * CORES:(r + 1) * CORES], near[lo:lo + CORES], far[lo:lo + CORES]))

    mine = exchange([jnp.stack(both) for both in zip(summed, turn(pieces, y - x))], along_x)
    other = jnp.stack([jnp.where(c == 0, piece[:, 1], piece[:, 0]) for piece in mine])
    other = along_sub(other, lambda zz, xx, cc: zz * TEAM + xx * CORES + 1 - cc)

    return pl.pallas_call(
        lay_kernel,
        in_specs=[ANY] * (LINE + 1),
        out_specs=ANY,
        out_shape=jax.ShapeDtypeStruct((beams, LINE * CORES * 2 * width), bf16),
        scratch_shapes=[
            pltpu.VMEM((beams, LINE * CORES * 2 * width), bf16),
            pltpu.SemaphoreType.DMA((2 * CORES * LINE,)),
            pltpu.SemaphoreType.DMA,
        ],
        compiler_params=pltpu.CompilerParams(vmem_limit_bytes=4 * 2**20),
        name="lay",
    )(*mine, other)


def solution(mesh):
    placed = (P("grp", None, None, "sub"), P(), P(), P(), P(None, "grp", None, None, None))
    return jax.shard_map(
        body, mesh=mesh, in_specs=placed, out_specs=P("sub", "grp"), check_vma=False
    )
```
